32 devices in a mesh: team: 4 (over y, core), tm: 8 (over z, x).
Axes of the slice: x: 2, y: 2, z: 4, core: 2. Of those that a mesh axis runs over, the one named last changes fastest.
Arguments:
- transitions: float32 [4, 8, 512, 512], P('team', 'tm'), may hold values from -0.25 to 1.25
- states: float32 [4, 8, 64, 512], P('team', 'tm'), may hold values from -1 to 1
- cotangent: float32 [4, 8, 64, 512], P('team', 'tm'), may hold values from -2.4 to 2.4
- terminal: float32 [4, 64, 512], P('team'), may hold values from -6 to 6
- incidence: int32 [4, 8, 32, 2048], P('team', 'tm'), may hold values 0 or 1
- measured: float32 [4, 8, 64, 32], P('team', 'tm'), may hold values from -0.12 to 0.12
- obs_gain: float32 [4, 512], P('team'), may hold values from -6 to 6
Outputs:
- adjoint: float32 [4, 8, 64, 512], P('team', 'tm')
- grad_transitions: bfloat16 [4, 8, 512, 512], P('team', 'tm')
The draws below stay inside these ranges and needn't reach their ends.
All inputs are finite; a program needn't handle non-finite values. No bound on the sum of `incidence` on one device may be relied on, other than what follows from the above.
Results may differ from the reference program's by a relative error of at most 0.001.
Values sent between devices are 32-bit elements; how exact they have to be, the bound alone decides.
A program may use at most 64 MiB of HBM per device.

```python
import math
import jax
import jax.numpy as jnp
from jax import lax

ROBOTS = 32
STATES = 16
TEAM_STATES = 512
COLS = 64
LMK = 2048
ROBOT_TEAMS = 4
WINDOW_STEPS = 8


def draw_transitions(key, part):
    random_keys = jax.random.split(key, 4)
    full_shape = (ROBOT_TEAMS, WINDOW_STEPS, TEAM_STATES, TEAM_STATES)
    noise = jnp.clip(jax.random.normal(random_keys[0], full_shape, jnp.float32), -4.0, 4.0)
    rate_low = 0.8
    spread = 0.3
    baseline_rate = jnp.exp(jax.random.uniform(random_keys[1], (ROBOT_TEAMS, 1, TEAM_STATES), jnp.float32, math.log(rate_low), math.log(0.995)))
    spike_event = jax.random.randint(random_keys[2], (ROBOT_TEAMS, WINDOW_STEPS, TEAM_STATES), 0, 32) == 0
    spike_factor = jnp.where(spike_event, jax.random.uniform(random_keys[3], (ROBOT_TEAMS, WINDOW_STEPS, TEAM_STATES), jnp.float32, 0.5, 0.8), 1.0)
    diagonal_part = baseline_rate * spike_factor
    unit_matrix = jnp.eye(TEAM_STATES, dtype=jnp.float32)
    return noise * (spread / math.sqrt(TEAM_STATES)) + diagonal_part[..., None] * unit_matrix


def with_ends(array, own_key, smallest, high):
    index_at = [jax.random.randint(jax.random.fold_in(own_key, axis), (), 0, length) for axis, length in enumerate(array.shape)]
    widest = array.shape.index(max(array.shape))
    beside = index_at[:widest] + [(index_at[widest] + 1) % array.shape[widest]] + index_at[widest + 1:]
    return array.at[tuple(index_at)].set(smallest).at[tuple(beside)].set(high)


def block_scale(rng, extent, cuts, smallest, largest):
    gain = 1.0
    for position, shards_of in cuts:
        heights = jax.random.uniform(jax.random.fold_in(jax.random.fold_in(rng, 6), position), (shards_of,), jnp.float32, smallest / len(cuts), largest / len(cuts))
        gain = gain * jnp.repeat(jnp.exp(heights), extent[position] // shards_of).reshape((-1,) + (1,) * (len(extent) - 1 - position))
    return gain


def centred(rng, dims, scale, reach, cuts=(), kind=jnp.bfloat16):
    array = jax.random.normal(rng, dims, jnp.float32) * scale
    if len(cuts) > 0:
        array = block_scale(rng, dims, cuts, -0.22, 0.18) * array
    return jnp.clip(array, min=-reach, max=reach).astype(kind)


def setup_inputs(seed: int = 0) -> dict:
    keys = jax.random.split(jax.random.key(seed), 8)
    return {
        "transitions": draw_transitions(jax.random.fold_in(keys[7], 71), 0),
        "states": centred(keys[1], (ROBOT_TEAMS, WINDOW_STEPS, COLS, TEAM_STATES), 0.125, 1.0, ((0, 4), (1, 8)), jnp.float32),
        "cotangent": centred(keys[2], (ROBOT_TEAMS, WINDOW_STEPS, COLS, TEAM_STATES), 0.3, 2.4, ((0, 4), (1, 8)), jnp.float32),
        "terminal": centred(keys[3], (ROBOT_TEAMS, COLS, TEAM_STATES), 1.0, 6.0, ((0, 4),), jnp.float32),
        "incidence": with_ends((jax.random.randint(keys[4], (ROBOT_TEAMS, WINDOW_STEPS, ROBOTS, LMK), 0, LMK) < 64).astype(jnp.int32), jax.random.fold_in(keys[4], 1), 0, 1),
        "measured": centred(keys[5], (ROBOT_TEAMS, WINDOW_STEPS, COLS, ROBOTS), 0.015, 0.12, ((0, 4), (1, 8)), jnp.float32),
        "obs_gain": centred(keys[6], (ROBOT_TEAMS, TEAM_STATES), 1.0, 6.0, ((0, 4),), jnp.float32),
    }


HIGHEST = lax.Precision.HIGHEST


def reference(transitions, states, cotangent, terminal, incidence, measured, obs_gain):
    incident = incidence.astype(jnp.float32)
    landmark = jnp.einsum('ktcr,ktrl->tcl', measured, incident, precision=HIGHEST)
    injection = jnp.einsum('tcl,ktrl->ktcr', landmark, incident, precision=HIGHEST)
    driven = cotangent + jnp.repeat(injection, STATES, axis=3) * obs_gain[:, None, None, :]

    def one_team(team_data):
        matrices, forward, forcing, final_cot = team_data

        def sweep_step(adjoint_next, pieces):
            matrix_now, state_now, force_now = pieces
            grad_now = jnp.einsum('cn,cm->nm', adjoint_next, state_now, precision=HIGHEST)
            adjoint_now = jnp.dot(adjoint_next, matrix_now, precision=HIGHEST) + force_now
            return adjoint_now, (adjoint_now, grad_now.astype(jnp.bfloat16))

        _, outputs = lax.scan(sweep_step, final_cot, (matrices, forward, forcing), reverse=True)
        return outputs

    adjoint, grad_transitions = lax.map(one_team, (transitions, states, driven, terminal))
    return adjoint, grad_transitions
```

```python
import functools

import jax
import jax.numpy as jnp
from jax import lax
from jax.experimental import pallas as pl
from jax.experimental.pallas import tpu as pltpu
from jax.sharding import PartitionSpec as P

CHUNKS = 4
F32 = jnp.float32
BF16 = jnp.bfloat16
MESH = pl.DeviceIdType.MESH


def split(value):
    high = value.astype(BF16)
    return high, (value - high.astype(F32)).astype(BF16)


def dot(left, right, dims=((1,), (0,))):
    return lax.dot_general(left, right, (dims, ((), ())), preferred_element_type=F32)


def kernel(
    teams, steps, chunks,
    t_hbm, s_hbm, cot_hbm, term_hbm, inc_hbm, meas_hbm, gain_hbm,
    adj_hbm, grad_hbm,
    t_vm, s_vm, gain_vm, th, tl, s3, x3, xin, drv, out, grad,
    meas, inc, part, parts,
    local_sem, inc_send, inc_recv, meas_send, meas_recv, part_send, part_recv,
    x_send, x_recv, out_sem, grad_sem,
):
    me = lax.axis_index("team")
    step = lax.axis_index("tm")
    last = step == steps - 1
    first = step == 0
    cols, width = xin.shape
    robots, cut = inc.shape[1:]
    rows = cols // chunks
    peers = [lax.rem(me + d, teams) for d in range(teams)]
    behind = [lax.rem(me + teams - d, teams) for d in range(teams)]

    barrier = pltpu.get_barrier_semaphore()
    for d in range(1, teams):
        pl.semaphore_signal(barrier, inc=1, device_id={"team": peers[d]}, device_id_type=MESH)

    @pl.when(step > 0)
    def _():
        pl.semaphore_signal(barrier, inc=1, device_id={"tm": step - 1}, device_id_type=MESH)

    @pl.when(step < steps - 1)
    def _():
        pl.semaphore_signal(barrier, inc=1, device_id={"tm": step + 1}, device_id_type=MESH)

    def columns(owner):
        return inc_hbm.at[0, 0, :, pl.ds(pl.multiple_of(owner * cut, cut), cut)]

    loads = [
        pltpu.make_async_copy(t_hbm.at[0, 0], t_vm, local_sem.at[0]),
        pltpu.make_async_copy(cot_hbm.at[0, 0], drv, local_sem.at[1]),
        pltpu.make_async_copy(s_hbm.at[0, 0], s_vm, local_sem.at[2]),
        pltpu.make_async_copy(meas_hbm.at[0, 0], meas.at[0], local_sem.at[3]),
        pltpu.make_async_copy(gain_hbm, gain_vm, local_sem.at[4]),
        pltpu.make_async_copy(columns(me), inc.at[0], local_sem.at[5]),
    ]
    for load in loads:
        load.start()
    terminal = pltpu.make_async_copy(term_hbm.at[0], xin, local_sem.at[6])

    @pl.when(last)
    def _():
        terminal.start()

    inc_copies = [None] + [
        pltpu.make_async_remote_copy(
            src_ref=columns(peers[d]), dst_ref=inc.at[d],
            send_sem=inc_send.at[d], recv_sem=inc_recv.at[d],
            device_id={"team": peers[d]}, device_id_type=MESH)
        for d in range(1, teams)
    ]
    meas_copies = [None] + [
        pltpu.make_async_remote_copy(
            src_ref=meas_hbm.at[0, 0], dst_ref=meas.at[d],
            send_sem=meas_send.at[d], recv_sem=meas_recv.at[d],
            device_id={"team": peers[d]}, device_id_type=MESH)
        for d in range(1, teams)
    ]
    neighbours = (step > 0).astype(jnp.int32) + (step < steps - 1).astype(jnp.int32)
    pl.semaphore_wait(barrier, teams - 1 + neighbours)
    for d in range(1, teams):
        meas_copies[d].start()
        inc_copies[d].start()

    loads[0].wait()

    @pl.loop(0, width // 64)
    def _(i):
        band = pl.ds(pl.multiple_of(i * 64, 64), 64)
        high, low = split(t_vm[band, :])
        th[band, :] = high
        tl[band, :] = low

    loads[1].wait()
    loads[2].wait()
    high, low = split(s_vm[...])
    s3[0:cols, :] = high
    s3[cols:2 * cols, :] = high
    s3[2 * cols:3 * cols, :] = low

    def times_transition(high, low):
        both = jnp.concatenate([high, low], axis=0)
        wide = dot(both, th[...])
        n = high.shape[0]
        return wide[:n] + wide[n:] + dot(high, tl[...])

    def keep(at, n, high, low):
        x3[at:at + n, :] = high
        x3[cols + at:cols + at + n, :] = low
        x3[2 * cols + at:2 * cols + at + n, :] = high

    @pl.when(last)
    def _():
        terminal.wait()
        high, low = split(xin[...])
        keep(0, cols, high, low)
        drv[...] += times_transition(high, low)

    loads[3].wait()
    loads[4].wait()
    loads[5].wait()
    landmark = jnp.zeros((2 * cols, cut), F32)
    seen = []
    for d in range(teams):
        if d:
            meas_copies[d].wait_recv()
            inc_copies[d].wait_recv()
        seen.append(inc[d].astype(F32).astype(BF16))
        high, low = split(meas[d])
        landmark = landmark + dot(jnp.concatenate([high, low], axis=0), seen[d])
    high, low = split(landmark[:cols] + landmark[cols:])
    both = jnp.concatenate([high, low], axis=0)
    part_copies = [None]
    for d in range(teams):
        piece = dot(both, seen[d], ((1,), (1,)))
        piece = piece[:cols] + piece[cols:]
        if d == 0:
            parts[0] = piece
            continue
        part[d] = piece
        copy = pltpu.make_async_remote_copy(
            src_ref=part.at[d], dst_ref=parts.at[d],
            send_sem=part_send.at[d], recv_sem=part_recv.at[d],
            device_id={"team": behind[d]}, device_id_type=MESH)
        copy.start()
        part_copies.append(copy)

    states = width // robots
    robot = lax.broadcasted_iota(jnp.int32, (robots, width), 0)
    state = lax.broadcasted_iota(jnp.int32, (robots, width), 1)
    lower = robot * states
    pick = jnp.where((state >= lower) & (state < lower + states), 1.0, 0.0).astype(BF16)
    injection = parts[0]
    for d in range(1, teams):
        part_copies[d].wait_recv()
        injection = injection + parts[d]
    high, low = split(injection)
    spread = dot(jnp.concatenate([high, low], axis=0), pick)
    drv[...] += (spread[:cols] + spread[cols:]) * gain_vm[...]

    x_copies = [
        pltpu.make_async_remote_copy(
            src_ref=out.at[pl.ds(i * rows, rows)], dst_ref=xin.at[pl.ds(i * rows, rows)],
            send_sem=x_send.at[i], recv_sem=x_recv.at[i],
            device_id={"tm": lax.max(step - 1, 0)}, device_id_type=MESH)
        for i in range(chunks)
    ]
    out_copies = [
        pltpu.make_async_copy(
            out.at[pl.ds(i * rows, rows)], adj_hbm.at[0, 0, pl.ds(i * rows, rows)], out_sem.at[i])
        for i in range(chunks)
    ]
    for i in range(chunks):
        at = i * rows

        @pl.when(last)
        def _():
            out[at:at + rows, :] = drv[at:at + rows, :]

        @pl.when(step < steps - 1)
        def _():
            x_copies[i].wait_recv()
            high, low = split(xin[at:at + rows, :])
            out[at:at + rows, :] = times_transition(high, low) + drv[at:at + rows, :]
            keep(at, rows, high, low)

        @pl.when(step > 0)
        def _():
            x_copies[i].start()

        out_copies[i].start()

    blocks = grad_sem.shape[0]
    high = width // blocks
    grad_copies = []
    for b in range(blocks):
        band = slice(b * high, (b + 1) * high)
        grad[band, :] = dot(x3[:, band], s3[...], ((0,), (0,))).astype(BF16)
        copy = pltpu.make_async_copy(
            grad.at[pl.ds(b * high, high)], grad_hbm.at[0, 0, pl.ds(b * high, high)], grad_sem.at[b])
        copy.start()
        grad_copies.append(copy)

    for d in range(1, teams):
        inc_copies[d].wait_send()
        meas_copies[d].wait_send()
        part_copies[d].wait_send()

    @pl.when(step > 0)
    def _():
        for copy in x_copies:
            copy.wait_send()

    for copy in out_copies + grad_copies:
        copy.wait()


def shards(teams, steps, transitions, states, cotangent, terminal, incidence, measured, obs_gain):
    cols, width = terminal.shape[1:]
    robots, landmarks = incidence.shape[2:]
    cut = landmarks // teams
    chunks = CHUNKS
    blocks = 4
    dma = pltpu.SemaphoreType.DMA
    anywhere = pl.BlockSpec(memory_space=pl.ANY)
    return pl.pallas_call(
        functools.partial(kernel, teams, steps, chunks),
        out_shape=(
            jax.ShapeDtypeStruct((1, 1, cols, width), F32),
            jax.ShapeDtypeStruct((1, 1, width, width), BF16),
        ),
        in_specs=[anywhere] * 7,
        out_specs=(anywhere, anywhere),
        scratch_shapes=[
            pltpu.VMEM((width, width), F32),
            pltpu.VMEM((cols, width), F32),
            pltpu.VMEM((1, width), F32),
            pltpu.VMEM((width, width), BF16),
            pltpu.VMEM((width, width), BF16),
            pltpu.VMEM((3 * cols, width), BF16),
            pltpu.VMEM((3 * cols, width), BF16),
            pltpu.VMEM((cols, width), F32),
            pltpu.VMEM((cols, width), F32),
            pltpu.VMEM((cols, width), F32),
            pltpu.VMEM((width, width), BF16),
            pltpu.VMEM((teams, cols, robots), F32),
            pltpu.VMEM((teams, robots, cut), jnp.int32),
            pltpu.VMEM((teams, cols, robots), F32),
            pltpu.VMEM((teams, cols, robots), F32),
            dma((7,)),
            dma((teams,)), dma((teams,)), dma((teams,)), dma((teams,)), dma((teams,)), dma((teams,)),
            dma((chunks,)), dma((chunks,)), dma((chunks,)), dma((blocks,)),
        ],
        compiler_params=pltpu.CompilerParams(
            collective_id=0, has_side_effects=True, vmem_limit_bytes=32 * 1024 * 1024),
    )(transitions, states, cotangent, terminal, incidence, measured, obs_gain)


def solution(mesh):
    placed = (
        P("team", "tm", None, None),
        P("team", "tm", None, None),
        P("team", "tm", None, None),
        P("team", None, None),
        P("team", "tm", None, None),
        P("team", "tm", None, None),
        P("team", None),
    )
    return jax.shard_map(
        functools.partial(shards, mesh.shape["team"], mesh.shape["tm"]),
        mesh=mesh,
        in_specs=placed,
        out_specs=(P("team", "tm", None, None), P("team", "tm", None, None)),
        check_vma=False,
    )
```

```python
import functools

import jax
import jax.numpy as jnp
from jax import lax
from jax.experimental import pallas as pl
from jax.experimental.pallas import tpu as pltpu
from jax.sharding import PartitionSpec as P

CHUNKS = 4
F32 = jnp.float32
BF16 = jnp.bfloat16
MESH = pl.DeviceIdType.MESH


def split(value):
    high = value.astype(BF16)
    return high, (value - high.astype(F32)).astype(BF16)


def dot(left, right, dims=((1,), (0,))):
    return lax.dot_general(left, right, (dims, ((), ())), preferred_element_type=F32)


def kernel(
    teams, steps, chunks, slabs,
    t_hbm, s_hbm, cot_hbm, term_hbm, inc_hbm, meas_hbm, gain_hbm,
    out, grad,
    t_vm, s_vm, gain_vm, th, tl, s3, x3, xin, adj,
    meas, inc, part, parts,
    local_sem, inc_send, inc_recv, meas_send, meas_recv, part_send, part_recv,
    fwd_send, x_send, x_recv, cot_sem, t_send, t_recv,
):
    me = lax.axis_index("team")
    step = lax.axis_index("tm")
    odd = lax.rem(step, 2)
    even = 1 - odd
    partner = step + 1 - 2 * odd
    side = lax.rem(me, 2)
    paired = step < steps - 2
    leader = paired & (side == odd)
    helper = paired & (side == even)
    ended = step == steps - 1
    hands_on = leader | jnp.logical_not(paired)
    skips = (step >= 2) & (leader | ((step == steps - 2) & (side == 0)))
    forwards = (step > 0) & hands_on
    slot = lax.max(odd, leader.astype(jnp.int32))
    cols, width = xin.shape
    robots, cut = inc.shape[1:]
    rows = cols // chunks
    peers = [lax.rem(me + d, teams) for d in range(teams)]
    behind = [lax.rem(me + teams - d, teams) for d in range(teams)]

    barrier = pltpu.get_barrier_semaphore()

    def greet(team, at):
        pl.semaphore_signal(barrier, inc=1, device_id={"team": team, "tm": at}, device_id_type=MESH)

    for d in range(teams):
        if d:
            greet(peers[d], step)
        greet(peers[d], partner)
    met = 2 * teams - 1
    beside = step - 1 + 2 * odd
    for at in (beside, step - 2, step + 2):
        inside = (at >= 0) & (at < steps)

        @pl.when(inside)
        def _():
            greet(me, at)

        met = met + inside.astype(jnp.int32)

    def columns(owner):
        return inc_hbm.at[0, 0, :, pl.ds(pl.multiple_of(owner * cut, cut), cut)]

    loads = [
        pltpu.make_async_copy(t_hbm.at[0, 0], t_vm.at[odd], local_sem.at[0]),
        pltpu.make_async_copy(cot_hbm.at[0, 0], adj.at[odd], local_sem.at[1]),
        pltpu.make_async_copy(s_hbm.at[0, 0], s_vm, local_sem.at[2]),
        pltpu.make_async_copy(meas_hbm.at[0, 0], meas.at[0], local_sem.at[3]),
        pltpu.make_async_copy(gain_hbm, gain_vm, local_sem.at[4]),
        pltpu.make_async_copy(columns(me), inc.at[0], local_sem.at[5]),
    ]
    for load in loads:
        load.start()
    terminal = pltpu.make_async_copy(term_hbm.at[0], xin, local_sem.at[6])

    @pl.when(ended)
    def _():
        terminal.start()

    def remote(src, dst, send, recv, team, at):
        return pltpu.make_async_remote_copy(
            src_ref=src, dst_ref=dst, send_sem=send, recv_sem=recv,
            device_id={"team": team, "tm": at}, device_id_type=MESH)

    inc_copies = [
        remote(columns(peers[d]), inc.at[d], inc_send.at[d], inc_recv.at[d], peers[d], step)
        for d in range(1, teams)
    ]
    meas_copies = [
        remote(meas_hbm.at[0, 0], meas.at[d], meas_send.at[d], meas_recv.at[d], peers[d], step)
        for d in range(1, teams)
    ]
    slab = width // slabs
    t_copies = [
        remote(t_hbm.at[0, 0, pl.ds(i * slab, slab)], t_vm.at[odd, pl.ds(i * slab, slab)],
               t_send.at[i], t_recv.at[i], me, partner)
        for i in range(slabs)
    ]
    t_arrivals = [
        remote(t_hbm.at[0, 0, pl.ds(i * slab, slab)], t_vm.at[even, pl.ds(i * slab, slab)],
               t_send.at[i], t_recv.at[i], me, partner)
        for i in range(slabs)
    ]
    cot_copy = remote(cot_hbm.at[0, 0], adj.at[odd], cot_sem.at[0], cot_sem.at[1], me, partner)
    cot_arrival = remote(cot_hbm.at[0, 0], adj.at[even], cot_sem.at[0], cot_sem.at[1], me, partner)

    pl.semaphore_wait(barrier, met)
    for copy in meas_copies + inc_copies:
        copy.start()

    @pl.when(helper)
    def _():
        cot_copy.start()
        for copy in t_copies:
            copy.start()

    def divide(which, start, stop):
        @pl.loop(start // 64, stop // 64)
        def _(i):
            band = pl.ds(pl.multiple_of(i * 64, 64), 64)
            high, low = split(t_vm[which, band, :])
            th[which, band, :] = high
            tl[which, band, :] = low

    loads[0].wait()
    divide(odd, 0, width)
    loads[1].wait()
    loads[2].wait()
    high, low = split(s_vm[...])
    s3[0:cols, :] = high
    s3[cols:2 * cols, :] = high
    s3[2 * cols:3 * cols, :] = low

    def times_transition(which, high, low):
        both = jnp.concatenate([high, low], axis=0)
        wide = dot(both, th[which])
        n = high.shape[0]
        return wide[:n] + wide[n:] + dot(high, tl[which])

    def keep(at, n, high, low):
        x3[at:at + n, :] = high
        x3[cols + at:cols + at + n, :] = low
        x3[2 * cols + at:2 * cols + at + n, :] = high

    loads[3].wait()
    loads[4].wait()
    loads[5].wait()
    landmark = jnp.zeros((2 * cols, cut), F32)
    seen = []
    for d in range(teams):
        if d:
            meas_copies[d - 1].wait_recv()
            inc_copies[d - 1].wait_recv()
        seen.append(inc[d].astype(F32).astype(BF16))
        high, low = split(meas[d])
        landmark = landmark + dot(jnp.concatenate([high, low], axis=1), seen[d], ((0,), (0,)))
    high, low = split(landmark[:cols] + landmark[cols:])
    both = jnp.concatenate([high, low], axis=0)

    def part_copy(d, parity, which, at):
        return remote(
            part.at[d], parts.at[parity, d], part_send.at[which, d], part_recv.at[parity, d], behind[d], at)

    for d in range(teams):
        piece = dot(both, seen[d], ((1,), (1,)))
        piece = piece[:cols] + piece[cols:]
        part[d] = piece
        if d:
            part_copy(d, odd, 0, step).start()
        else:
            parts[odd, 0] = piece

        @pl.when(paired & (lax.rem(behind[d], 2) == even))
        def _():
            part_copy(d, odd, 1, partner).start()

    @pl.when(ended)
    def _():
        terminal.wait()
        high, low = split(xin[...])
        adj[1] += times_transition(1, high, low)

        keep(0, cols, high, low)

    states = width // robots
    robot = lax.broadcasted_iota(jnp.int32, (robots, width), 0)
    state = lax.broadcasted_iota(jnp.int32, (robots, width), 1)
    lower = robot * states
    pick = jnp.where((state >= lower) & (state < lower + states), 1.0, 0.0).astype(BF16)

    def inject(parity, first):
        for d in range(first, teams):
            part_copy(d, parity, 0, step).wait_recv()
        injection = parts[parity, 0]
        for d in range(1, teams):
            injection = injection + parts[parity, d]
        high, low = split(injection)
        spread = dot(jnp.concatenate([high, low], axis=0), pick)
        adj[parity] += (spread[:cols] + spread[cols:]) * gain_vm[...]

    inject(odd, 1)

    @pl.when(leader)
    def _():
        cot_arrival.wait_recv()
        inject(even, 0)
        for i in range(slabs):
            t_arrivals[i].wait_recv()
            divide(even, i * slab, (i + 1) * slab)

    def band(i):
        return pl.ds(i * rows, rows)

    x_copies = [
        remote(adj.at[0, band(i)], xin.at[band(i)], x_send.at[i], x_recv.at[i], me, lax.max(step - 2, 0))
        for i in range(chunks)
    ]
    fwd_copies = [
        remote(adj.at[odd, band(i)], xin.at[band(i)], fwd_send.at[i], x_recv.at[i], me, lax.max(step - 1, 0))
        for i in range(chunks)
    ]
    for i in range(chunks):
        at = i * rows

        @pl.when(jnp.logical_not(ended))
        def _():
            x_copies[i].wait_recv()
            high, low = split(xin[at:at + rows, :])
            adj[slot, at:at + rows, :] += times_transition(slot, high, low)

            @pl.when(slot == odd)
            def _():
                keep(at, rows, high, low)

        @pl.when(forwards & (odd == 1))
        def _():
            fwd_copies[i].start()

        @pl.when(leader)
        def _():
            high, low = split(adj[1, at:at + rows, :])
            adj[0, at:at + rows, :] += times_transition(0, high, low)

            @pl.when(odd == 0)
            def _():
                keep(at, rows, high, low)

        @pl.when(skips)
        def _():
            x_copies[i].start()

        @pl.when(forwards & (odd == 0))
        def _():
            fwd_copies[i].start()

    blocks = 4
    high = width // blocks
    for b in range(blocks):
        at = slice(b * high, (b + 1) * high)
        grad[0, 0, at, :] = dot(x3[:, at], s3[...], ((0,), (0,))).astype(BF16)
    out[0, 0] = adj[odd]

    for copy in meas_copies + inc_copies:
        copy.wait_send()
    for d in range(teams):
        if d:
            part_copy(d, odd, 0, step).wait_send()

        @pl.when(paired & (lax.rem(behind[d], 2) == even))
        def _():
            part_copy(d, odd, 1, partner).wait_send()

    @pl.when(helper)
    def _():
        for copy in t_copies:
            copy.wait_send()
        cot_copy.wait_send()

    @pl.when(skips)
    def _():
        for copy in x_copies:
            copy.wait_send()

    @pl.when(forwards)
    def _():
        for copy in fwd_copies:
            copy.wait_send()


def shards(teams, steps, transitions, states, cotangent, terminal, incidence, measured, obs_gain):
    cols, width = terminal.shape[1:]
    robots, landmarks = incidence.shape[2:]
    cut = landmarks // teams
    chunks = CHUNKS
    slabs = 1
    dma = pltpu.SemaphoreType.DMA
    remote = pl.BlockSpec(memory_space=pltpu.HBM)
    local = pl.BlockSpec(memory_space=pltpu.VMEM)
    return pl.pallas_call(
        functools.partial(kernel, teams, steps, chunks, slabs),
        out_shape=(
            jax.ShapeDtypeStruct((1, 1, cols, width), F32),
            jax.ShapeDtypeStruct((1, 1, width, width), BF16),
        ),
        in_specs=[remote] * 7,
        out_specs=(local, local),
        scratch_shapes=[
            pltpu.VMEM((2, width, width), F32),
            pltpu.VMEM((cols, width), F32),
            pltpu.VMEM((1, width), F32),
            pltpu.VMEM((2, width, width), BF16),
            pltpu.VMEM((2, width, width), BF16),
            pltpu.VMEM((3 * cols, width), BF16),
            pltpu.VMEM((3 * cols, width), BF16),
            pltpu.VMEM((cols, width), F32),
            pltpu.VMEM((2, cols, width), F32),
            pltpu.VMEM((teams, robots, cols), F32),
            pltpu.VMEM((teams, robots, cut), jnp.int32),
            pltpu.VMEM((teams, cols, robots), F32),
            pltpu.VMEM((2, teams, cols, robots), F32),
            dma((7,)),
            dma((teams,)), dma((teams,)), dma((teams,)), dma((teams,)),
            dma((2, teams)), dma((2, teams)),
            dma((chunks,)), dma((chunks,)), dma((chunks,)),
            dma((2,)), dma((slabs,)), dma((slabs,)),
        ],
        compiler_params=pltpu.CompilerParams(
            collective_id=0, has_side_effects=True, vmem_limit_bytes=63 * 1024 * 1024),
    )(transitions, states, cotangent, terminal, incidence, jnp.swapaxes(measured, 2, 3), obs_gain)


def solution(mesh):
    placed = (
        P("team", "tm", None, None),
        P("team", "tm", None, None),
        P("team", "tm", None, None),
        P("team", None, None),
        P("team", "tm", None, None),
        P("team", "tm", None, None),
        P("team", None),
    )
    return jax.shard_map(
        functools.partial(shards, mesh.shape["team"], mesh.shape["tm"]),
        mesh=mesh,
        in_specs=placed,
        out_specs=(P("team", "tm", None, None), P("team", "tm", None, None)),
        check_vma=False,
    )
```

```python
import functools

import jax
import jax.numpy as jnp
from jax import lax
from jax.experimental import pallas as pl
from jax.experimental.pallas import tpu as pltpu
from jax.sharding import PartitionSpec as P

CHUNKS = 4
F32 = jnp.float32
BF16 = jnp.bfloat16
MESH = pl.DeviceIdType.MESH


def split(value):
    high = value.astype(BF16)
    return high, (value - high.astype(F32)).astype(BF16)


def dot(left, right, dims=((1,), (0,))):
    return lax.dot_general(left, right, (dims, ((), ())), preferred_element_type=F32)


def kernel(
    teams, steps, chunks, slabs,
    t_hbm, s_hbm, cot_hbm, term_hbm, inc_hbm, meas_hbm, gain_hbm,
    out, x3, s3,
    t_vm, s_vm, gain_vm, th, tl, xin, adj,
    meas, inc, part, parts,
    local_sem, inc_send, inc_recv, meas_send, meas_recv, part_send, part_recv,
    fwd_send, x_send, x_recv, cot_sem, t_send, t_recv,
):
    me = lax.axis_index("team")
    step = lax.axis_index("tm")
    odd = lax.rem(step, 2)
    even = 1 - odd
    partner = step + 1 - 2 * odd
    side = lax.rem(me, 2)
    paired = step < steps - 4
    leader = paired & (side == odd)
    helper = paired & (side == even)
    ended = step == steps - 1
    hands_on = leader | jnp.logical_not(paired)
    skips = (step >= 2) & (leader | ((step == steps - 4) & (side == 0)))
    forwards = (step > 0) & hands_on
    slot = lax.max(odd, leader.astype(jnp.int32))
    cols, width = xin.shape
    robots, cut = inc.shape[1:]
    rows = cols // chunks
    peers = [lax.rem(me + d, teams) for d in range(teams)]
    behind = [lax.rem(me + teams - d, teams) for d in range(teams)]

    barrier = pltpu.get_barrier_semaphore()

    def greet(team, at):
        pl.semaphore_signal(barrier, inc=1, device_id={"team": team, "tm": at}, device_id_type=MESH)

    for d in range(teams):
        if d:
            greet(peers[d], step)
        greet(peers[d], partner)
    met = 2 * teams - 1
    beside = step - 1 + 2 * odd
    for at in (beside, step - 2, step + 2):
        inside = (at >= 0) & (at < steps)

        @pl.when(inside)
        def _():
            greet(me, at)

        met = met + inside.astype(jnp.int32)

    def columns(owner):
        return inc_hbm.at[0, 0, :, pl.ds(pl.multiple_of(owner * cut, cut), cut)]

    loads = [
        pltpu.make_async_copy(t_hbm.at[0, 0], t_vm.at[odd], local_sem.at[0]),
        pltpu.make_async_copy(cot_hbm.at[0, 0], adj.at[odd], local_sem.at[1]),
        pltpu.make_async_copy(s_hbm.at[0, 0], s_vm, local_sem.at[2]),
        pltpu.make_async_copy(meas_hbm.at[0, 0], meas.at[0], local_sem.at[3]),
        pltpu.make_async_copy(gain_hbm, gain_vm, local_sem.at[4]),
        pltpu.make_async_copy(columns(me), inc.at[0], local_sem.at[5]),
    ]
    for load in loads:
        load.start()
    terminal = pltpu.make_async_copy(term_hbm.at[0], xin, local_sem.at[6])

    @pl.when(ended)
    def _():
        terminal.start()

    def remote(src, dst, send, recv, team, at):
        return pltpu.make_async_remote_copy(
            src_ref=src, dst_ref=dst, send_sem=send, recv_sem=recv,
            device_id={"team": team, "tm": at}, device_id_type=MESH)

    inc_copies = [
        remote(columns(peers[d]), inc.at[d], inc_send.at[d], inc_recv.at[d], peers[d], step)
        for d in range(1, teams)
    ]
    meas_copies = [
        remote(meas_hbm.at[0, 0], meas.at[d], meas_send.at[d], meas_recv.at[d], peers[d], step)
        for d in range(1, teams)
    ]
    slab = width // slabs
    t_copies = [
        remote(t_hbm.at[0, 0, pl.ds(i * slab, slab)], t_vm.at[odd, pl.ds(i * slab, slab)],
               t_send.at[i], t_recv.at[i], me, partner)
        for i in range(slabs)
    ]
    t_arrivals = [
        remote(t_hbm.at[0, 0, pl.ds(i * slab, slab)], t_vm.at[even, pl.ds(i * slab, slab)],
               t_send.at[i], t_recv.at[i], me, partner)
        for i in range(slabs)
    ]
    cot_copy = remote(cot_hbm.at[0, 0], adj.at[odd], cot_sem.at[0], cot_sem.at[1], me, partner)
    cot_arrival = remote(cot_hbm.at[0, 0], adj.at[even], cot_sem.at[0], cot_sem.at[1], me, partner)

    pl.semaphore_wait(barrier, met)
    for copy in meas_copies + inc_copies:
        copy.start()

    @pl.when(helper)
    def _():
        cot_copy.start()
        for copy in t_copies:
            copy.start()

    def divide(which, start, stop):
        @pl.loop(start // 64, stop // 64)
        def _(i):
            band = pl.ds(pl.multiple_of(i * 64, 64), 64)
            high, low = split(t_vm[which, band, :])
            th[which, band, :] = high
            tl[which, band, :] = low

    loads[0].wait()
    divide(odd, 0, width)
    loads[1].wait()
    loads[2].wait()
    high, low = split(s_vm[...])
    s3[0:cols, :] = high
    s3[cols:2 * cols, :] = high
    s3[2 * cols:3 * cols, :] = low

    def times_transition(which, high, low):
        both = jnp.concatenate([high, low], axis=0)
        wide = dot(both, th[which])
        n = high.shape[0]
        return wide[:n] + wide[n:] + dot(high, tl[which])

    def keep(at, n, high, low):
        x3[at:at + n, :] = high
        x3[cols + at:cols + at + n, :] = low
        x3[2 * cols + at:2 * cols + at + n, :] = high

    loads[3].wait()
    loads[4].wait()
    loads[5].wait()
    landmark = jnp.zeros((2 * cols, cut), F32)
    seen = []
    for d in range(teams):
        if d:
            meas_copies[d - 1].wait_recv()
            inc_copies[d - 1].wait_recv()
        seen.append(inc[d].astype(F32).astype(BF16))
        high, low = split(meas[d])
        landmark = landmark + dot(jnp.concatenate([high, low], axis=1), seen[d], ((0,), (0,)))
    high, low = split(landmark[:cols] + landmark[cols:])
    both = jnp.concatenate([high, low], axis=0)

    def part_copy(d, parity, which, at):
        return remote(
            part.at[d], parts.at[parity, d], part_send.at[which, d], part_recv.at[parity, d], behind[d], at)

    for d in range(teams):
        piece = dot(both, seen[d], ((1,), (1,)))
        piece = piece[:cols] + piece[cols:]
        part[d] = piece
        if d:
            part_copy(d, odd, 0, step).start()
        else:
            parts[odd, 0] = piece

        @pl.when(paired & (lax.rem(behind[d], 2) == even))
        def _():
            part_copy(d, odd, 1, partner).start()

    @pl.when(ended)
    def _():
        terminal.wait()
        high, low = split(xin[...])
        adj[1] += times_transition(1, high, low)

        keep(0, cols, high, low)

    states = width // robots
    robot = lax.broadcasted_iota(jnp.int32, (robots, width), 0)
    state = lax.broadcasted_iota(jnp.int32, (robots, width), 1)
    lower = robot * states
    pick = jnp.where((state >= lower) & (state < lower + states), 1.0, 0.0).astype(BF16)

    def inject(parity, first):
        for d in range(first, teams):
            part_copy(d, parity, 0, step).wait_recv()
        injection = parts[parity, 0]
        for d in range(1, teams):
            injection = injection + parts[parity, d]
        high, low = split(injection)
        spread = dot(jnp.concatenate([high, low], axis=0), pick)
        adj[parity] += (spread[:cols] + spread[cols:]) * gain_vm[...]

    inject(odd, 1)

    @pl.when(leader)
    def _():
        cot_arrival.wait_recv()
        inject(even, 0)
        for i in range(slabs):
            t_arrivals[i].wait_recv()
            divide(even, i * slab, (i + 1) * slab)

    def band(i):
        return pl.ds(i * rows, rows)

    x_copies = [
        remote(adj.at[0, band(i)], xin.at[band(i)], x_send.at[i], x_recv.at[i], me, lax.max(step - 2, 0))
        for i in range(chunks)
    ]
    fwd_copies = [
        remote(adj.at[odd, band(i)], xin.at[band(i)], fwd_send.at[i], x_recv.at[i], me, lax.max(step - 1, 0))
        for i in range(chunks)
    ]
    for i in range(chunks):
        at = i * rows

        @pl.when(jnp.logical_not(ended))
        def _():
            x_copies[i].wait_recv()
            high, low = split(xin[at:at + rows, :])
            adj[slot, at:at + rows, :] += times_transition(slot, high, low)

            @pl.when(slot == odd)
            def _():
                keep(at, rows, high, low)

        @pl.when(forwards & (odd == 1))
        def _():
            fwd_copies[i].start()

        @pl.when(leader)
        def _():
            high, low = split(adj[1, at:at + rows, :])
            adj[0, at:at + rows, :] += times_transition(0, high, low)

            @pl.when(odd == 0)
            def _():
                keep(at, rows, high, low)

        @pl.when(skips)
        def _():
            x_copies[i].start()

        @pl.when(forwards & (odd == 0))
        def _():
            fwd_copies[i].start()

    out[0, 0] = adj[odd]

    for copy in meas_copies + inc_copies:
        copy.wait_send()
    for d in range(teams):
        if d:
            part_copy(d, odd, 0, step).wait_send()

        @pl.when(paired & (lax.rem(behind[d], 2) == even))
        def _():
            part_copy(d, odd, 1, partner).wait_send()

    @pl.when(helper)
    def _():
        for copy in t_copies:
            copy.wait_send()
        cot_copy.wait_send()

    @pl.when(skips)
    def _():
        for copy in x_copies:
            copy.wait_send()

    @pl.when(forwards)
    def _():
        for copy in fwd_copies:
            copy.wait_send()


def shards(teams, steps, transitions, states, cotangent, terminal, incidence, measured, obs_gain):
    cols, width = terminal.shape[1:]
    robots, landmarks = incidence.shape[2:]
    cut = landmarks // teams
    chunks = CHUNKS
    slabs = 1
    dma = pltpu.SemaphoreType.DMA
    remote = pl.BlockSpec(memory_space=pltpu.HBM)
    local = pl.BlockSpec(memory_space=pltpu.VMEM)
    adjoint, x3, s3 = pl.pallas_call(
        functools.partial(kernel, teams, steps, chunks, slabs),
        out_shape=(
            jax.ShapeDtypeStruct((1, 1, cols, width), F32),
            jax.ShapeDtypeStruct((3 * cols, width), BF16),
            jax.ShapeDtypeStruct((3 * cols, width), BF16),
        ),
        in_specs=[remote] * 7,
        out_specs=(local, local, local),
        scratch_shapes=[
            pltpu.VMEM((2, width, width), F32),
            pltpu.VMEM((cols, width), F32),
            pltpu.VMEM((1, width), F32),
            pltpu.VMEM((2, width, width), BF16),
            pltpu.VMEM((2, width, width), BF16),
            pltpu.VMEM((cols, width), F32),
            pltpu.VMEM((2, cols, width), F32),
            pltpu.VMEM((teams, robots, cols), F32),
            pltpu.VMEM((teams, robots, cut), jnp.int32),
            pltpu.VMEM((teams, cols, robots), F32),
            pltpu.VMEM((2, teams, cols, robots), F32),
            dma((7,)),
            dma((teams,)), dma((teams,)), dma((teams,)), dma((teams,)),
            dma((2, teams)), dma((2, teams)),
            dma((chunks,)), dma((chunks,)), dma((chunks,)),
            dma((2,)), dma((slabs,)), dma((slabs,)),
        ],
        compiler_params=pltpu.CompilerParams(
            collective_id=0, has_side_effects=True, vmem_limit_bytes=63 * 1024 * 1024),
    )(transitions, states, cotangent, terminal, incidence, jnp.swapaxes(measured, 2, 3), obs_gain)
    grad = dot(x3, s3, ((0,), (0,))).astype(BF16)
    return adjoint, grad[None, None]


def solution(mesh):
    placed = (
        P("team", "tm", None, None),
        P("team", "tm", None, None),
        P("team", "tm", None, None),
        P("team", None, None),
        P("team", "tm", None, None),
        P("team", "tm", None, None),
        P("team", None),
    )
    return jax.shard_map(
        functools.partial(shards, mesh.shape["team"], mesh.shape["tm"]),
        mesh=mesh,
        in_specs=placed,
        out_specs=(P("team", "tm", None, None), P("team", "tm", None, None)),
        check_vma=False,
    )
```
